512 devices in a mesh: tm: 32 (over y, z_lo), height: 16 (over x, z_hi, core).
Axes of the slice: x: 4, y: 4, z: 16 (z_hi: 2, z_lo: 8; z = z_hi * 8 + z_lo), core: 2. Of those that a mesh axis runs over, the one named last changes fastest.
Arguments:
- queries: bfloat16 [64, 48, 32, 2560], P('tm', 'height'), may hold values from -8 to 8
- keys_values: bfloat16 [2, 64, 48, 32, 2560], P(None, 'tm', 'height'), may hold values from -8 to 8
- anchor_ids: int32 [96], replicated, may hold values from 0 to 1535, as said below
Outputs:
- attended: bfloat16 [64, 48, 32, 2560], P('tm', 'height')
The draws below stay inside these ranges and needn't reach their ends.
Inputs may be any that keep to these rules, and one draw needn't show every extreme that they name: `anchor_ids`: anchor j lies in tile j: tiles of 4 x 4 tokens of frame 0 in row-major order, 8 a tile row; the first tile's anchor is its first token and the last tile's its last token.
All inputs are finite; a program needn't handle non-finite values.
Results may differ from the reference program's by a relative error of at most 0.0033.
Values may be sent and summed in bfloat16 or wider, within the bound.
A program may use at most 128 MiB of HBM per device.

```python
import jax
import jax.numpy as jnp
from jax import lax

COLS = 32
HEADS = 20
FEAT = 2560
TFR = 64
ROWS = 48


def draw_queries(key, part):
    key = jax.random.fold_in(key, 11)
    shape = (TFR, ROWS, COLS, FEAT)
    base = jnp.clip(2.0 * jax.random.normal(key, shape, jnp.float32), -8.0, 8.0)
    return base.astype(jnp.bfloat16)


def draw_keys_values(key, part):
    key = jax.random.fold_in(key, 12)
    shape = (2, TFR, ROWS, COLS, FEAT)
    base = jnp.clip(jax.random.normal(key, shape, jnp.float32), -8.0, 8.0)
    return base.astype(jnp.bfloat16)


def draw_anchor_ids(key, part):
    key = jax.random.fold_in(key, 13)
    tile_rows = ROWS // 4
    tile_cols = COLS // 4
    key_row, key_col = jax.random.split(key)
    shift_row = jax.random.randint(key_row, (tile_rows, tile_cols), 0, 4)
    shift_col = jax.random.randint(key_col, (tile_rows, tile_cols), 0, 4)
    shift_row = shift_row.at[0, 0].set(0).at[tile_rows - 1, tile_cols - 1].set(3)
    shift_col = shift_col.at[0, 0].set(0).at[tile_rows - 1, tile_cols - 1].set(3)
    row = 4 * jnp.arange(tile_rows, dtype=jnp.int32)[:, None] + shift_row
    col = 4 * jnp.arange(tile_cols, dtype=jnp.int32)[None, :] + shift_col
    return (row * COLS + col).reshape(-1).astype(jnp.int32)


def setup_inputs(seed: int = 0) -> dict:
    splits = jax.random.split(jax.random.key(seed), 4)
    queries = draw_queries(jax.random.fold_in(splits[3], 71), 0)
    keys_values = draw_keys_values(jax.random.fold_in(splits[3], 71), 0)
    anchor_ids = draw_anchor_ids(jax.random.fold_in(splits[3], 71), 0)
    return {"queries": queries, "keys_values": keys_values, "anchor_ids": anchor_ids}


def reference(queries, keys_values, anchor_ids):
    tfr, rows, cols, feat = queries.shape
    heads = HEADS
    head_dim = feat // heads
    scale = 1.0 / (head_dim ** 0.5)
    first_flat = keys_values[:, 0].reshape(2, rows * cols, feat)
    anchors = jnp.take(first_flat, anchor_ids, axis=1)
    anchor_keys = anchors[0].reshape(-1, heads, head_dim).astype(jnp.float32)
    anchor_vals = anchors[1].reshape(-1, heads, head_dim).astype(jnp.float32)
    col_iota = jnp.arange(cols, dtype=jnp.int32)
    col_near = jnp.abs(col_iota[None, :] - col_iota[:, None]) <= 3

    def one_band(index):
        frame = (index // rows).astype(jnp.int32)
        row = (index % rows).astype(jnp.int32)
        frame_start = jnp.clip(frame - 1, 0, tfr - 3).astype(jnp.int32)
        row_start = jnp.clip(row - 3, 0, rows - 7).astype(jnp.int32)
        zero = jnp.zeros((), jnp.int32)
        query_band = lax.dynamic_slice(queries, (frame, row, zero, zero), (1, 1, cols, feat))
        query_band = query_band.reshape(cols, heads, head_dim).astype(jnp.float32)
        key_block = lax.dynamic_slice(keys_values, (zero, frame_start, row_start, zero, zero), (2, 3, 7, cols, feat))
        key_block = key_block.reshape(2, 3 * 7 * cols, heads, head_dim).astype(jnp.float32)
        key_frames = frame_start + jnp.arange(3, dtype=jnp.int32)
        key_rows = row_start + jnp.arange(7, dtype=jnp.int32)
        frame_ok = jnp.abs(key_frames - frame) <= 1
        row_ok = jnp.abs(key_rows - row) <= 3
        allowed = frame_ok[None, :, None, None] & row_ok[None, None, :, None] & col_near[:, None, None, :]
        allowed = allowed.reshape(cols, 3 * 7 * cols)
        local_scores = jnp.einsum("qhd,khd->hqk", query_band, key_block[0]) * scale
        local_scores = jnp.where(allowed[None], local_scores, -1e30)
        anchor_scores = jnp.einsum("qhd,ahd->hqa", query_band, anchor_keys) * scale
        top = jnp.maximum(jnp.max(local_scores, axis=-1), jnp.max(anchor_scores, axis=-1))
        local_weights = jnp.exp(local_scores - top[..., None])
        anchor_weights = jnp.exp(anchor_scores - top[..., None])
        total = jnp.sum(local_weights, axis=-1) + jnp.sum(anchor_weights, axis=-1)
        local_round = lax.optimization_barrier(local_weights.astype(jnp.bfloat16)).astype(jnp.float32)
        anchor_round = lax.optimization_barrier(anchor_weights.astype(jnp.bfloat16)).astype(jnp.float32)
        summed = jnp.einsum("hqk,khd->qhd", local_round, key_block[1])
        summed = summed + jnp.einsum("hqa,ahd->qhd", anchor_round, anchor_vals)
        result = summed / jnp.transpose(total)[:, :, None]
        return result.reshape(cols, feat).astype(jnp.bfloat16)

    bands = lax.map(one_band, jnp.arange(tfr * rows, dtype=jnp.int32))
    return bands.reshape(tfr, rows, cols, feat)
```

```python
import functools

import jax
import jax.numpy as jnp
from jax import lax
from jax.experimental import pallas as pl
from jax.experimental.pallas import tpu as pltpu
from jax.sharding import PartitionSpec as P

HEADS = 20
GROUPS = 5
REACH = 3
LOG2E = 1.4426950408889634
MASKED = -1e30
MESH = pl.DeviceIdType.MESH

CORE, UP, DOWN, PASS_UP, PASS_DOWN, QUERY = 0, 2, 4, 6, 8, 10
PART = QUERY + GROUPS
STAT = PART + GROUPS
TRANSFERS = STAT + GROUPS


def attention_kernel(
    frames, rows, cols, tm_count, height_count,
    queries, keys_values, anchors, out,
    own, mate, own_queries, far_queries, sent_part, far_part, sent_stat, far_stat,
    result, own_level, near_bias, cross_bias, stat_block, send_sem, recv_sem, local_sem,
):
    band = rows * cols
    tokens = frames * band
    feat = queries.shape[1]
    size = feat // HEADS
    per_group = HEADS // GROUPS
    width = per_group * size
    scale = LOG2E / size**0.5

    time_index = lax.axis_index("tm")
    height_index = lax.axis_index("height")
    core = lax.rem(height_index, 2)
    has_down = time_index > 0
    has_up = time_index < tm_count - 1
    has_far = ((core == 0) & (height_index > 0)) | ((core == 1) & (height_index < height_count - 1))
    core_mate = (time_index, height_index + 1 - 2 * core)
    far_mate = (time_index, jnp.clip(height_index - 1 + 2 * core, 0, height_count - 1))
    below = (jnp.maximum(time_index - 1, 0), height_index)
    above = (jnp.minimum(time_index + 1, tm_count - 1), height_index)

    barrier = pltpu.get_barrier_semaphore()
    pl.semaphore_signal(barrier, inc=1, device_id=core_mate, device_id_type=MESH)
    for exists, mate_id in ((has_down, below), (has_up, above), (has_far, far_mate)):

        @pl.when(exists)
        def _():
            pl.semaphore_signal(barrier, inc=1, device_id=mate_id, device_id_type=MESH)

    peers = 1 + sum(exists.astype(jnp.int32) for exists in (has_down, has_up, has_far))
    pl.semaphore_wait(barrier, peers)

    def remote(index, src, dst, device):
        return pltpu.make_async_remote_copy(
            src_ref=src, dst_ref=dst, send_sem=send_sem.at[index], recv_sem=recv_sem.at[index],
            device_id=device, device_id_type=MESH,
        )

    first, last = pl.ds(0, band), pl.ds(tokens + band, band)
    middle = pl.ds(band, tokens)

    def share(kv):
        return remote(CORE + kv, keys_values.at[kv], mate.at[kv, middle], core_mate)

    def send_up(kv):
        src = keys_values.at[kv, pl.ds(tokens - band, band)]
        return remote(UP + kv, src, own.at[kv, first], above)

    def send_down(kv):
        return remote(DOWN + kv, keys_values.at[kv, pl.ds(0, band)], own.at[kv, last], below)

    def pass_first(kv):
        return remote(PASS_UP + kv, own.at[kv, first], mate.at[kv, first], core_mate)

    def pass_last(kv):
        return remote(PASS_DOWN + kv, own.at[kv, last], mate.at[kv, last], core_mate)

    def columns(group):
        return pl.ds(group * width, width)

    def send_query(group):
        cut = columns(group)
        return remote(QUERY + group, queries.at[:, cut], far_queries.at[:, cut], far_mate)

    def send_part(group):
        cut = columns(group)
        return remote(PART + group, sent_part.at[:, cut], far_part.at[:, cut], far_mate)

    def send_stat(group):
        return remote(STAT + group, sent_stat.at[group], far_stat.at[group], far_mate)

    copies = [pltpu.make_async_copy(queries, own_queries, local_sem.at[2])]
    for kv in range(2):
        copies.append(
            pltpu.make_async_copy(keys_values.at[kv], own.at[kv, middle], local_sem.at[kv])
        )
    for copy in copies:
        copy.start()
    for kv in range(2):
        share(kv).start()

    @pl.when(has_up)
    def _():
        for kv in range(2):
            send_up(kv).start()

    @pl.when(has_down)
    def _():
        for kv in range(2):
            send_down(kv).start()

    @pl.when(has_far)
    def _():
        for group in range(GROUPS):
            send_query(group).start()

    @pl.when(jnp.logical_not(has_down))
    def _():
        for ref in (own, mate):
            ref[:, 0:band, :] = jnp.zeros((2, band, feat), ref.dtype)

    @pl.when(jnp.logical_not(has_up))
    def _():
        for ref in (own, mate):
            ref[:, tokens + band : tokens + 2 * band, :] = jnp.zeros((2, band, feat), ref.dtype)

    @pl.when(jnp.logical_not(has_far))
    def _():
        far_part[...] = jnp.zeros(far_part.shape, far_part.dtype)
        far_stat[...] = jnp.full(far_stat.shape, MASKED, far_stat.dtype)

    span = 3 * band
    query_token = lax.broadcasted_iota(jnp.int32, (band, span), 0)
    key_token = lax.broadcasted_iota(jnp.int32, (band, span), 1)
    query_row, query_col = query_token // cols, lax.rem(query_token, cols)
    key_frame = key_token // band
    key_row = lax.rem(key_token, band) // cols
    key_col = lax.rem(key_token, cols)
    near = jnp.abs(query_col - key_col) <= REACH
    behind = jnp.where(core == 0, query_row - key_row, key_row - query_row)
    for frame in range(frames):
        moment = time_index * frames + frame - 1 + key_frame
        valid = near & (moment >= 0) & (moment < tm_count * frames)
        near_bias[frame] = jnp.where(valid, 0.0, MASKED)
        cross_bias[frame] = jnp.where(valid & (behind >= 0), 0.0, MASKED)

    @pl.when(has_down)
    def _():
        for kv in range(2):
            send_up(kv).wait_recv()
            pass_first(kv).start()

    @pl.when(has_up)
    def _():
        for kv in range(2):
            send_down(kv).wait_recv()
            pass_last(kv).start()

    for copy in copies:
        copy.wait()

    def scores(query, keys):
        return scale * lax.dot_general(
            query, keys, (((1,), (1,)), ((), ())), preferred_element_type=jnp.float32
        )

    def weighted(weights, values):
        return jnp.dot(weights.astype(values.dtype), values, preferred_element_type=jnp.float32)

    lane = lax.broadcasted_iota(jnp.int32, (band, size), 1)

    def far_block(group, step):
        head, frame = step // frames, lax.rem(step, frames)
        cut = pl.ds(pl.multiple_of((group * per_group + head) * size, size), size)
        here = pl.ds(pl.multiple_of(frame * band, band), band)
        around = pl.ds(pl.multiple_of(frame * band, band), span)
        score = scores(far_queries[here, cut], own[0, around, cut]) + cross_bias[frame]
        top = jnp.max(score, axis=1, keepdims=True)
        weights = jnp.exp2(score - top)
        total = jnp.sum(weights, axis=1, keepdims=True)
        part = weighted(weights, own[1, around, cut]) / total
        sent_part[here, cut] = part.astype(sent_part.dtype)
        level = top + jnp.log(total) * LOG2E
        stat_block[here, :] = jnp.where(lane == head, level, stat_block[here, :])

    @pl.when(has_far)
    def _():
        stat_block[...] = jnp.zeros(stat_block.shape, stat_block.dtype)
        for group in range(GROUPS):
            send_query(group).wait_recv()

            @pl.loop(0, frames * per_group)
            def _(step):
                far_block(group, step)

            sent_stat[group] = jnp.transpose(stat_block[...])[0:8]
            send_part(group).start()
            send_stat(group).start()

    for kv in range(2):
        share(kv).wait_recv()

    @pl.when(has_down)
    def _():
        for kv in range(2):
            pass_first(kv).wait_recv()

    @pl.when(has_up)
    def _():
        for kv in range(2):
            pass_last(kv).wait_recv()

    @pl.loop(0, frames * HEADS)
    def _(step):
        head, frame = step // frames, lax.rem(step, frames)
        cut = pl.ds(pl.multiple_of(head * size, size), size)
        here = pl.ds(pl.multiple_of(frame * band, band), band)
        around = pl.ds(pl.multiple_of(frame * band, band), span)
        query = own_queries[here, cut]
        near_score = scores(query, own[0, around, cut]) + near_bias[frame]
        cross_score = scores(query, mate[0, around, cut]) + cross_bias[frame]
        anchor_score = scores(query, anchors[0, :, cut])
        top = jnp.maximum(
            jnp.maximum(
                jnp.max(near_score, axis=1, keepdims=True),
                jnp.max(cross_score, axis=1, keepdims=True),
            ),
            jnp.max(anchor_score, axis=1, keepdims=True),
        )
        near_weights = jnp.exp2(near_score - top)
        cross_weights = jnp.exp2(cross_score - top)
        anchor_weights = jnp.exp2(anchor_score - top)
        total = (
            jnp.sum(near_weights, axis=1, keepdims=True)
            + jnp.sum(cross_weights, axis=1, keepdims=True)
            + jnp.sum(anchor_weights, axis=1, keepdims=True)
        )
        summed = (
            weighted(near_weights, own[1, around, cut])
            + weighted(cross_weights, mate[1, around, cut])
            + weighted(anchor_weights, anchors[1, :, cut])
        )
        result[here, cut] = summed / total
        own_level[here, cut] = jnp.broadcast_to(top + jnp.log(total) * LOG2E, (band, size))

    for group in range(GROUPS):

        @pl.when(has_far)
        def _():
            send_part(group).wait_recv()
            send_stat(group).wait_recv()

        stats = jnp.transpose(far_stat[group])
        for head in range(per_group):
            cut = pl.ds((group * per_group + head) * size, size)
            far_level = stats[0:tokens, head : head + 1]
            mine = own_level[:, cut]
            top = jnp.maximum(mine, far_level)
            mine = jnp.exp2(mine - top)
            other = jnp.exp2(far_level - top)
            mixed = mine * result[:, cut] + other * far_part[:, cut].astype(jnp.float32)
            out[:, cut] = (mixed / (mine + other)).astype(out.dtype)

    for kv in range(2):
        share(kv).wait_send()

    @pl.when(has_up)
    def _():
        for kv in range(2):
            send_up(kv).wait_send()
            pass_last(kv).wait_send()

    @pl.when(has_down)
    def _():
        for kv in range(2):
            send_down(kv).wait_send()
            pass_first(kv).wait_send()

    @pl.when(has_far)
    def _():
        for group in range(GROUPS):
            send_query(group).wait_send()
            send_part(group).wait_send()
            send_stat(group).wait_send()


def per_device(tm_count, height_count, queries, keys_values, anchor_ids):
    frames, rows, cols, feat = queries.shape
    band = rows * cols
    tokens = frames * band
    size = feat // HEADS
    padded = -(-tokens // 128) * 128
    time_index = lax.axis_index("tm")
    row_index = lax.axis_index("height")
    local_tokens = row_index * band + jnp.arange(band, dtype=jnp.int32)
    first_flat = keys_values[:, 0].reshape(2, band, feat)
    selector = (anchor_ids[:, None] == local_tokens[None, :]) & (time_index == 0)
    selector = selector.astype(jnp.bfloat16)
    picked = jnp.einsum("an,snf->saf", selector, first_flat, preferred_element_type=jnp.float32)
    anchors = lax.psum(picked, ("tm", "height")).astype(jnp.bfloat16)

    kernel = functools.partial(attention_kernel, frames, rows, cols, tm_count, height_count)
    bf16, f32 = jnp.bfloat16, jnp.float32
    out = pl.pallas_call(
        kernel,
        out_shape=jax.ShapeDtypeStruct((tokens, feat), bf16),
        in_specs=[
            pl.BlockSpec(memory_space=pl.ANY),
            pl.BlockSpec(memory_space=pl.ANY),
            pl.BlockSpec(memory_space=pltpu.VMEM),
        ],
        out_specs=pl.BlockSpec(memory_space=pltpu.VMEM),
        scratch_shapes=[
            pltpu.VMEM((2, tokens + 2 * band, feat), bf16),
            pltpu.VMEM((2, tokens + 2 * band, feat), bf16),
            pltpu.VMEM((tokens, feat), bf16),
            pltpu.VMEM((tokens, feat), bf16),
            pltpu.VMEM((tokens, feat), bf16),
            pltpu.VMEM((tokens, feat), bf16),
            pltpu.VMEM((GROUPS, 8, padded), f32),
            pltpu.VMEM((GROUPS, 8, padded), f32),
            pltpu.VMEM((tokens, feat), f32),
            pltpu.VMEM((tokens, feat), f32),
            pltpu.VMEM((frames, band, 3 * band), f32),
            pltpu.VMEM((frames, band, 3 * band), f32),
            pltpu.VMEM((padded, size), f32),
            pltpu.SemaphoreType.DMA((TRANSFERS,)),
            pltpu.SemaphoreType.DMA((TRANSFERS,)),
            pltpu.SemaphoreType.DMA((3,)),
        ],
        compiler_params=pltpu.CompilerParams(
            collective_id=0, has_side_effects=True, vmem_limit_bytes=48 * 1024 * 1024
        ),
        name="attention",
    )(queries.reshape(tokens, feat), keys_values.reshape(2, tokens, feat), anchors)
    return out.reshape(frames, rows, cols, feat)


def solution(mesh):
    body = functools.partial(per_device, mesh.shape["tm"], mesh.shape["height"])
    return jax.shard_map(
        body,
        mesh=mesh,
        in_specs=(P("tm", "height", None, None), P(None, "tm", "height", None, None), P()),
        out_specs=P("tm", "height", None, None),
        check_vma=False,
    )
```

```python
import functools

import jax
import jax.numpy as jnp
from jax import lax
from jax.experimental import pallas as pl
from jax.experimental.pallas import tpu as pltpu
from jax.sharding import PartitionSpec as P

HEADS = 20
GROUPS = 5
REACH = 3
LOG2E = 1.4426950408889634
MASKED = -1e30
MESH = pl.DeviceIdType.MESH

CORE, UP, DOWN, PASS_UP, PASS_DOWN, QUERY = 0, 2, 4, 6, 8, 10
PART = QUERY + GROUPS
STAT = PART + GROUPS
JOIN = STAT + GROUPS
SCATTER = JOIN + 2
SPREAD = SCATTER + 4
ALONG_Y = SPREAD + 8
ALONG_X = ALONG_Y + 4
TO_MATE = ALONG_X + 4
TRANSFERS = TO_MATE + 4

XS, YS, Z_LO = 4, 4, 8
SLOT = 32


def attention_kernel(
    frames, rows, cols, tm_count, height_count,
    queries, keys_values, anchor_ids, out,
    own, mate, own_queries, far_queries, sent_part, far_part, sent_stat, far_stat,
    result, own_level, near_bias, cross_bias, stat_block,
    partial, mate_partial, far_partial, picked, anchors, send_sem, recv_sem, local_sem,
):
    band = rows * cols
    tokens = frames * band
    feat = queries.shape[1]
    size = feat // HEADS
    per_group = HEADS // GROUPS
    width = per_group * size
    scale = LOG2E / size**0.5

    time_index = lax.axis_index("tm")
    height_index = lax.axis_index("height")
    core = lax.rem(height_index, 2)
    has_down = time_index > 0
    has_up = time_index < tm_count - 1
    has_far = ((core == 0) & (height_index > 0)) | ((core == 1) & (height_index < height_count - 1))
    core_mate = (time_index, height_index + 1 - 2 * core)
    far_mate = (time_index, jnp.clip(height_index - 1 + 2 * core, 0, height_count - 1))
    below = (jnp.maximum(time_index - 1, 0), height_index)
    above = (jnp.minimum(time_index + 1, tm_count - 1), height_index)

    x, z_hi = height_index // 4, lax.rem(height_index // 2, 2)
    y, z_lo = time_index // Z_LO, lax.rem(time_index, Z_LO)
    source_hi = jnp.where(z_lo < Z_LO // 2, z_hi, 1 - z_hi)
    active = core == 1 - source_hi
    hub = active & (z_lo == 0)
    root = time_index == 0
    face = hub & root
    leaf = active & (z_lo != 0)
    y_peers = [(lax.rem(y + d, YS) * Z_LO + z_lo, height_index) for d in range(1, YS)]
    x_peers = [
        (time_index, (lax.rem(x + d, XS) * 2 + z_hi) * 2 + core) for d in range(1, XS)
    ]

    def at_z(z):
        return (y * Z_LO + lax.rem(z, Z_LO), (x * 2 + z // Z_LO) * 2 + core)

    leaves = [
        at_z(lax.rem(z_hi * Z_LO + d + 2 * Z_LO, 2 * Z_LO))
        for d in (-4, 3, -3, 2, -2, 1, -1)
    ]
    my_hub = at_z(source_hi * Z_LO)

    barrier = pltpu.get_barrier_semaphore()
    pl.semaphore_signal(barrier, inc=1, device_id=core_mate, device_id_type=MESH)
    for exists, mate_id in ((has_down, below), (has_up, above), (has_far, far_mate)):

        @pl.when(exists)
        def _():
            pl.semaphore_signal(barrier, inc=1, device_id=mate_id, device_id_type=MESH)

    for exists, group in ((active, y_peers + x_peers), (hub, leaves), (leaf, [my_hub])):

        @pl.when(exists)
        def _():
            for mate_id in group:
                pl.semaphore_signal(barrier, inc=1, device_id=mate_id, device_id_type=MESH)

    peers = 1 + sum(exists.astype(jnp.int32) for exists in (has_down, has_up, has_far, leaf))
    peers = peers + 6 * active.astype(jnp.int32) + 7 * hub.astype(jnp.int32)
    pl.semaphore_wait(barrier, peers)

    def remote(index, src, dst, device, arrival=None):
        arrival = index if arrival is None else arrival
        return pltpu.make_async_remote_copy(
            src_ref=src, dst_ref=dst, send_sem=send_sem.at[index], recv_sem=recv_sem.at[arrival],
            device_id=device, device_id_type=MESH,
        )

    first, last = pl.ds(0, band), pl.ds(tokens + band, band)
    middle = pl.ds(band, tokens)

    def share(kv):
        return remote(CORE + kv, keys_values.at[kv], mate.at[kv, middle], core_mate)

    def send_up(kv):
        src = keys_values.at[kv, pl.ds(tokens - band, band)]
        return remote(UP + kv, src, own.at[kv, first], above)

    def send_down(kv):
        return remote(DOWN + kv, keys_values.at[kv, pl.ds(0, band)], own.at[kv, last], below)

    def pass_first(kv):
        return remote(PASS_UP + kv, own.at[kv, first], mate.at[kv, first], core_mate)

    def pass_last(kv):
        return remote(PASS_DOWN + kv, own.at[kv, last], mate.at[kv, last], core_mate)

    def columns(group):
        return pl.ds(group * width, width)

    def send_query(group):
        cut = columns(group)
        return remote(QUERY + group, queries.at[:, cut], far_queries.at[:, cut], far_mate)

    def send_part(group):
        cut = columns(group)
        return remote(PART + group, sent_part.at[:, cut], far_part.at[:, cut], far_mate)

    def send_stat(group):
        return remote(STAT + group, sent_stat.at[group], far_stat.at[group], far_mate)

    def slot(index):
        return pl.ds(pl.multiple_of(index * SLOT, SLOT), SLOT)

    piece = feat // YS

    def quarter(index):
        return pl.ds(pl.multiple_of(index * piece, piece), piece)

    def join_core():
        return remote(JOIN, partial, mate_partial, core_mate)

    def join_far():
        return remote(JOIN + 1, partial, far_partial, far_mate)

    def scatter(d):
        cut = quarter(lax.rem(y + d, YS))
        src, dst = picked.at[:, :, cut], anchors.at[:, slot(x), cut]
        return remote(SCATTER + d, src, dst, y_peers[d - 1], SCATTER)

    def spread(index):
        here = anchors.at[:, slot(x), quarter(y)]
        return remote(SPREAD + index, here, here, leaves[index], SPREAD)

    def along_y(d, arriving=False):
        here = anchors.at[:, slot(x), quarter(lax.rem(y + YS - d, YS) if arriving else y)]
        return remote(ALONG_Y + d, here, here, y_peers[d - 1])

    def along_x(d, arriving=False):
        here = anchors.at[:, slot(lax.rem(x + XS - d, XS) if arriving else x)]
        return remote(ALONG_X + d, here, here, x_peers[d - 1])

    def to_mate(d):
        here = anchors.at[:, slot(lax.rem(x + XS - d, XS))]
        return remote(TO_MATE + d, here, here, core_mate)

    copies = [pltpu.make_async_copy(queries, own_queries, local_sem.at[2])]
    for kv in range(2):
        copies.append(
            pltpu.make_async_copy(keys_values.at[kv], own.at[kv, middle], local_sem.at[kv])
        )
    for copy in copies:
        copy.start()
    for kv in range(2):
        share(kv).start()

    @pl.when(has_up)
    def _():
        for kv in range(2):
            send_up(kv).start()

    @pl.when(has_down)
    def _():
        for kv in range(2):
            send_down(kv).start()

    @pl.when(has_far)
    def _():
        for group in range(GROUPS):
            send_query(group).start()

    @pl.when(root)
    def _():
        for kv in range(2):
            copies[1 + kv].wait()
        ids = anchor_ids[slot(x), :]
        token = lax.broadcasted_iota(jnp.int32, (SLOT, band), 1) + height_index * band
        selector = (ids[:, 0:band] == token).astype(partial.dtype)
        for kv in range(2):
            for part in range(YS):
                cut = slice(part * piece, (part + 1) * piece)
                partial[kv, :, cut] = jnp.dot(
                    selector, own[kv, band : 2 * band, cut], preferred_element_type=jnp.float32
                ).astype(partial.dtype)
        join_core().start()
        join_core().wait()
        for kv in range(2):
            picked[kv] = partial[kv] + mate_partial[kv]

    @pl.when(face)
    def _():
        for kv in range(2):
            partial[kv] = picked[kv]
        join_far().start()
        join_far().wait()
        for kv in range(2):
            picked[kv] = picked[kv] + far_partial[kv]
        for d in range(1, YS):
            scatter(d).start()
        anchors[:, slot(x), 0:piece] = picked[:, :, 0:piece]

    @pl.when(hub & jnp.logical_not(root))
    def _():
        scatter_arrived = anchors.at[:, slot(x), quarter(y)]
        remote(SCATTER, scatter_arrived, scatter_arrived, y_peers[0]).wait_recv()

    @pl.when(hub)
    def _():
        for index in range(7):
            spread(index).start()

    @pl.when(leaf)
    def _():
        spread(0).wait_recv()

    @pl.when(active)
    def _():
        for d in range(1, YS):
            along_y(d).start()
        for d in range(1, YS):
            along_y(d, True).wait_recv()
        for d in range(1, XS):
            along_x(d).start()
        to_mate(0).start()
        for d in range(1, XS):
            along_x(d, True).wait_recv()
            to_mate(d).start()

    @pl.when(jnp.logical_not(has_down))
    def _():
        for ref in (own, mate):
            ref[:, 0:band, :] = jnp.zeros((2, band, feat), ref.dtype)

    @pl.when(jnp.logical_not(has_up))
    def _():
        for ref in (own, mate):
            ref[:, tokens + band : tokens + 2 * band, :] = jnp.zeros((2, band, feat), ref.dtype)

    @pl.when(jnp.logical_not(has_far))
    def _():
        far_part[...] = jnp.zeros(far_part.shape, far_part.dtype)
        far_stat[...] = jnp.full(far_stat.shape, MASKED, far_stat.dtype)

    span = 3 * band
    query_token = lax.broadcasted_iota(jnp.int32, (band, span), 0)
    key_token = lax.broadcasted_iota(jnp.int32, (band, span), 1)
    query_row, query_col = query_token // cols, lax.rem(query_token, cols)
    key_frame = key_token // band
    key_row = lax.rem(key_token, band) // cols
    key_col = lax.rem(key_token, cols)
    near = jnp.abs(query_col - key_col) <= REACH
    behind = jnp.where(core == 0, query_row - key_row, key_row - query_row)
    for frame in range(frames):
        moment = time_index * frames + frame - 1 + key_frame
        valid = near & (moment >= 0) & (moment < tm_count * frames)
        near_bias[frame] = jnp.where(valid, 0.0, MASKED)
        cross_bias[frame] = jnp.where(valid & (behind >= 0), 0.0, MASKED)

    @pl.when(has_down)
    def _():
        for kv in range(2):
            send_up(kv).wait_recv()
            pass_first(kv).start()

    @pl.when(has_up)
    def _():
        for kv in range(2):
            send_down(kv).wait_recv()
            pass_last(kv).start()

    copies[0].wait()

    @pl.when(jnp.logical_not(root))
    def _():
        for kv in range(2):
            copies[1 + kv].wait()

    def scores(query, keys):
        return scale * lax.dot_general(
            query, keys, (((1,), (1,)), ((), ())), preferred_element_type=jnp.float32
        )

    def weighted(weights, values):
        return jnp.dot(weights.astype(values.dtype), values, preferred_element_type=jnp.float32)

    lane = lax.broadcasted_iota(jnp.int32, (band, size), 1)

    def far_block(group, step):
        head, frame = step // frames, lax.rem(step, frames)
        cut = pl.ds(pl.multiple_of((group * per_group + head) * size, size), size)
        here = pl.ds(pl.multiple_of(frame * band, band), band)
        around = pl.ds(pl.multiple_of(frame * band, band), span)
        score = scores(far_queries[here, cut], own[0, around, cut]) + cross_bias[frame]
        top = jnp.max(score, axis=1, keepdims=True)
        weights = jnp.exp2(score - top)
        total = jnp.sum(weights, axis=1, keepdims=True)
        part = weighted(weights, own[1, around, cut]) / total
        sent_part[here, cut] = part.astype(sent_part.dtype)
        level = top + jnp.log(total) * LOG2E
        stat_block[here, :] = jnp.where(lane == head, level, stat_block[here, :])

    @pl.when(has_far)
    def _():
        stat_block[...] = jnp.zeros(stat_block.shape, stat_block.dtype)
        for group in range(GROUPS):
            send_query(group).wait_recv()

            @pl.loop(0, frames * per_group)
            def _(step):
                far_block(group, step)

            sent_stat[group] = jnp.transpose(stat_block[...])[0:8]
            send_part(group).start()
            send_stat(group).start()

    for kv in range(2):
        share(kv).wait_recv()

    @pl.when(has_down)
    def _():
        for kv in range(2):
            pass_first(kv).wait_recv()

    @pl.when(has_up)
    def _():
        for kv in range(2):
            pass_last(kv).wait_recv()

    @pl.when(jnp.logical_not(active))
    def _():
        for d in range(XS):
            to_mate(d).wait_recv()

    held = lax.rem(lax.broadcasted_iota(jnp.int32, (1, XS * SLOT), 1), SLOT)
    anchor_bias = jnp.where(held < 24, 0.0, MASKED)

    @pl.loop(0, frames * HEADS)
    def _(step):
        head, frame = step // frames, lax.rem(step, frames)
        cut = pl.ds(pl.multiple_of(head * size, size), size)
        here = pl.ds(pl.multiple_of(frame * band, band), band)
        around = pl.ds(pl.multiple_of(frame * band, band), span)
        query = own_queries[here, cut]
        near_score = scores(query, own[0, around, cut]) + near_bias[frame]
        cross_score = scores(query, mate[0, around, cut]) + cross_bias[frame]
        anchor_score = scores(query, anchors[0, :, cut]) + anchor_bias
        top = jnp.maximum(
            jnp.maximum(
                jnp.max(near_score, axis=1, keepdims=True),
                jnp.max(cross_score, axis=1, keepdims=True),
            ),
            jnp.max(anchor_score, axis=1, keepdims=True),
        )
        near_weights = jnp.exp2(near_score - top)
        cross_weights = jnp.exp2(cross_score - top)
        anchor_weights = jnp.exp2(anchor_score - top)
        total = (
            jnp.sum(near_weights, axis=1, keepdims=True)
            + jnp.sum(cross_weights, axis=1, keepdims=True)
            + jnp.sum(anchor_weights, axis=1, keepdims=True)
        )
        summed = (
            weighted(near_weights, own[1, around, cut])
            + weighted(cross_weights, mate[1, around, cut])
            + weighted(anchor_weights, anchors[1, :, cut])
        )
        result[here, cut] = summed / total
        own_level[here, cut] = jnp.broadcast_to(top + jnp.log(total) * LOG2E, (band, size))

    for group in range(GROUPS):

        @pl.when(has_far)
        def _():
            send_part(group).wait_recv()
            send_stat(group).wait_recv()

        stats = jnp.transpose(far_stat[group])
        for head in range(per_group):
            cut = pl.ds((group * per_group + head) * size, size)
            far_level = stats[0:tokens, head : head + 1]
            mine = own_level[:, cut]
            top = jnp.maximum(mine, far_level)
            mine = jnp.exp2(mine - top)
            other = jnp.exp2(far_level - top)
            mixed = mine * result[:, cut] + other * far_part[:, cut].astype(jnp.float32)
            out[:, cut] = (mixed / (mine + other)).astype(out.dtype)

    for kv in range(2):
        share(kv).wait_send()

    @pl.when(has_up)
    def _():
        for kv in range(2):
            send_up(kv).wait_send()
            pass_last(kv).wait_send()

    @pl.when(has_down)
    def _():
        for kv in range(2):
            send_down(kv).wait_send()
            pass_first(kv).wait_send()

    @pl.when(face)
    def _():
        for d in range(1, YS):
            scatter(d).wait_send()

    @pl.when(hub)
    def _():
        for index in range(7):
            spread(index).wait_send()

    @pl.when(active)
    def _():
        for d in range(1, YS):
            along_y(d).wait_send()
        for d in range(1, XS):
            along_x(d).wait_send()
        for d in range(XS):
            to_mate(d).wait_send()

    @pl.when(has_far)
    def _():
        for group in range(GROUPS):
            send_query(group).wait_send()
            send_part(group).wait_send()
            send_stat(group).wait_send()


def per_device(tm_count, height_count, queries, keys_values, anchor_ids):
    frames, rows, cols, feat = queries.shape
    band = rows * cols
    tokens = frames * band
    size = feat // HEADS
    padded = -(-tokens // 128) * 128
    ids = jnp.pad(anchor_ids.reshape(XS, -1), ((0, 0), (0, SLOT - 24)), constant_values=-1)
    ids = jnp.broadcast_to(ids.reshape(XS * SLOT, 1), (XS * SLOT, 128))

    kernel = functools.partial(attention_kernel, frames, rows, cols, tm_count, height_count)
    bf16, f32 = jnp.bfloat16, jnp.float32
    out = pl.pallas_call(
        kernel,
        out_shape=jax.ShapeDtypeStruct((tokens, feat), bf16),
        in_specs=[
            pl.BlockSpec(memory_space=pl.ANY),
            pl.BlockSpec(memory_space=pl.ANY),
            pl.BlockSpec(memory_space=pltpu.VMEM),
        ],
        out_specs=pl.BlockSpec(memory_space=pltpu.VMEM),
        scratch_shapes=[
            pltpu.VMEM((2, tokens + 2 * band, feat), bf16),
            pltpu.VMEM((2, tokens + 2 * band, feat), bf16),
            pltpu.VMEM((tokens, feat), bf16),
            pltpu.VMEM((tokens, feat), bf16),
            pltpu.VMEM((tokens, feat), bf16),
            pltpu.VMEM((tokens, feat), bf16),
            pltpu.VMEM((GROUPS, 8, padded), f32),
            pltpu.VMEM((GROUPS, 8, padded), f32),
            pltpu.VMEM((tokens, feat), f32),
            pltpu.VMEM((tokens, feat), f32),
            pltpu.VMEM((frames, band, 3 * band), f32),
            pltpu.VMEM((frames, band, 3 * band), f32),
            pltpu.VMEM((padded, size), f32),
            pltpu.VMEM((2, SLOT, feat), bf16),
            pltpu.VMEM((2, SLOT, feat), bf16),
            pltpu.VMEM((2, SLOT, feat), bf16),
            pltpu.VMEM((2, SLOT, feat), bf16),
            pltpu.VMEM((2, XS * SLOT, feat), bf16),
            pltpu.SemaphoreType.DMA((TRANSFERS,)),
            pltpu.SemaphoreType.DMA((TRANSFERS,)),
            pltpu.SemaphoreType.DMA((3,)),
        ],
        compiler_params=pltpu.CompilerParams(
            collective_id=0, has_side_effects=True, vmem_limit_bytes=48 * 1024 * 1024
        ),
        name="attention",
    )(queries.reshape(tokens, feat), keys_values.reshape(2, tokens, feat), ids)
    return out.reshape(frames, rows, cols, feat)


def solution(mesh):
    body = functools.partial(per_device, mesh.shape["tm"], mesh.shape["height"])
    return jax.shard_map(
        body,
        mesh=mesh,
        in_specs=(P("tm", "height", None, None), P(None, "tm", "height", None, None), P()),
        out_specs=P("tm", "height", None, None),
        check_vma=False,
    )
```

```python
import functools

import jax
import jax.numpy as jnp
from jax import lax
from jax.experimental import pallas as pl
from jax.experimental.pallas import tpu as pltpu
from jax.sharding import PartitionSpec as P

HEADS = 20
GROUPS = 5
REACH = 3
LOG2E = 1.4426950408889634
MASKED = -1e30
MESH = pl.DeviceIdType.MESH

CORE, UP, DOWN, PASS_UP, PASS_DOWN, QUERY = 0, 2, 4, 6, 8, 10
PART = QUERY + GROUPS
STAT = PART + GROUPS
JOIN = STAT + GROUPS
SCATTER = JOIN + 2
SPREAD = SCATTER + 4
ALONG_Y = SPREAD + 8
ALONG_X = ALONG_Y + 4
TO_MATE = ALONG_X + 4
TRANSFERS = TO_MATE + 4

XS, YS, Z_LO = 4, 4, 8
SLOT = 32


def attention_kernel(
    frames, rows, cols, tm_count, height_count,
    queries, keys_values, anchor_ids, out,
    own, mate, own_queries, far_queries, sent_part, far_part, sent_stat, far_stat,
    result, own_level, near_bias, cross_bias, stat_block,
    partial, mate_partial, far_partial, picked, anchors, send_sem, recv_sem, local_sem,
):
    band = rows * cols
    tokens = frames * band
    feat = queries.shape[1]
    size = feat // HEADS
    per_group = HEADS // GROUPS
    width = per_group * size
    scale = LOG2E / size**0.5

    time_index = lax.axis_index("tm")
    height_index = lax.axis_index("height")
    core = lax.rem(height_index, 2)
    has_down = time_index > 0
    has_up = time_index < tm_count - 1
    has_far = ((core == 0) & (height_index > 0)) | ((core == 1) & (height_index < height_count - 1))
    core_mate = (time_index, height_index + 1 - 2 * core)
    far_mate = (time_index, jnp.clip(height_index - 1 + 2 * core, 0, height_count - 1))
    below = (jnp.maximum(time_index - 1, 0), height_index)
    above = (jnp.minimum(time_index + 1, tm_count - 1), height_index)

    bent = ((height_index == 4) | (height_index == height_count - 5))
    turn = jnp.logical_not(has_far)
    bend_end = (height_index == 3) | (height_index == height_count - 4)
    low = height_index < height_count // 2
    turn_id = (time_index, jnp.where(low, 0, height_count - 1))
    bent_id = (time_index, jnp.where(low, 4, height_count - 5))
    bend_end_id = (time_index, jnp.where(low, 3, height_count - 4))
    query_mate = (time_index, jnp.where(bent, turn_id[1], far_mate[1]))

    x, z_hi = height_index // 4, lax.rem(height_index // 2, 2)
    y, z_lo = time_index // Z_LO, lax.rem(time_index, Z_LO)
    active = core == 1 - z_hi
    hub = active & (z_lo == 0)
    root = time_index == 0
    face = hub & root
    leaf = active & (z_lo != 0)
    y_peers = [(lax.rem(y + d, YS) * Z_LO + z_lo, height_index) for d in range(1, YS)]
    x_peers = [
        (time_index, (lax.rem(x + d, XS) * 2 + z_hi) * 2 + core) for d in range(1, XS)
    ]

    leaves = [(y * Z_LO + d, height_index) for d in range(Z_LO - 1, 0, -1)]
    my_hub = (y * Z_LO, height_index)

    barrier = pltpu.get_barrier_semaphore()
    pl.semaphore_signal(barrier, inc=1, device_id=core_mate, device_id_type=MESH)
    for exists, mate_id in ((has_down, below), (has_up, above), (has_far, far_mate)):

        @pl.when(exists)
        def _():
            pl.semaphore_signal(barrier, inc=1, device_id=mate_id, device_id_type=MESH)

    for exists, group in (
        (active, y_peers + x_peers),
        (hub, leaves),
        (leaf, [my_hub]),
        (bent | bend_end, [turn_id]),
        (turn, [bent_id, bend_end_id]),
    ):

        @pl.when(exists)
        def _():
            for mate_id in group:
                pl.semaphore_signal(barrier, inc=1, device_id=mate_id, device_id_type=MESH)

    peers = 1 + sum(exists.astype(jnp.int32) for exists in (has_down, has_up, has_far, leaf))
    peers = peers + 6 * active.astype(jnp.int32) + 7 * hub.astype(jnp.int32)
    peers = peers + (bent | bend_end).astype(jnp.int32) + 2 * turn.astype(jnp.int32)
    pl.semaphore_wait(barrier, peers)

    def remote(index, src, dst, device, arrival=None):
        arrival = index if arrival is None else arrival
        return pltpu.make_async_remote_copy(
            src_ref=src, dst_ref=dst, send_sem=send_sem.at[index], recv_sem=recv_sem.at[arrival],
            device_id=device, device_id_type=MESH,
        )

    first, last = pl.ds(0, band), pl.ds(tokens + band, band)
    middle = pl.ds(band, tokens)

    def share(kv):
        return remote(CORE + kv, keys_values.at[kv], mate.at[kv, middle], core_mate)

    def send_up(kv):
        src = keys_values.at[kv, pl.ds(tokens - band, band)]
        return remote(UP + kv, src, own.at[kv, first], above)

    def send_down(kv):
        return remote(DOWN + kv, keys_values.at[kv, pl.ds(0, band)], own.at[kv, last], below)

    def pass_first(kv):
        return remote(PASS_UP + kv, own.at[kv, first], mate.at[kv, first], core_mate)

    def pass_last(kv):
        return remote(PASS_DOWN + kv, own.at[kv, last], mate.at[kv, last], core_mate)

    def columns(group):
        return pl.ds(group * width, width)

    def send_query(group):
        cut = columns(group)
        return remote(QUERY + group, queries.at[:, cut], far_queries.at[:, cut], query_mate)

    def turn_query(group):
        here = far_queries.at[:, columns(group)]
        return remote(QUERY + group, here, here, bend_end_id)

    def send_part(group):
        cut = columns(group)
        return remote(PART + group, sent_part.at[:, cut], far_part.at[:, cut], far_mate)

    def send_stat(group):
        return remote(STAT + group, sent_stat.at[group], far_stat.at[group], far_mate)

    def slot(index):
        return pl.ds(pl.multiple_of(index * SLOT, SLOT), SLOT)

    piece = feat // YS

    def quarter(index):
        return pl.ds(pl.multiple_of(index * piece, piece), piece)

    def join_core():
        return remote(JOIN, partial, mate_partial, core_mate)

    def join_far():
        return remote(JOIN + 1, partial, far_partial, far_mate)

    def scatter(d):
        cut = quarter(lax.rem(y + d, YS))
        src, dst = picked.at[:, :, cut], anchors.at[:, slot(x), cut]
        return remote(SCATTER + d, src, dst, y_peers[d - 1], SCATTER)

    def spread(index):
        here = anchors.at[:, slot(x), quarter(y)]
        return remote(SPREAD + index, here, here, leaves[index], SPREAD)

    def along_y(d, arriving=False):
        here = anchors.at[:, slot(x), quarter(lax.rem(y + YS - d, YS) if arriving else y)]
        return remote(ALONG_Y + d, here, here, y_peers[d - 1])

    def along_x(d, arriving=False):
        here = anchors.at[:, slot(lax.rem(x + XS - d, XS) if arriving else x)]
        return remote(ALONG_X + d, here, here, x_peers[d - 1])

    def to_mate(d):
        here = anchors.at[:, slot(lax.rem(x + XS - d, XS))]
        return remote(TO_MATE + d, here, here, core_mate)

    copies = [pltpu.make_async_copy(queries, own_queries, local_sem.at[2])]
    for kv in range(2):
        copies.append(
            pltpu.make_async_copy(keys_values.at[kv], own.at[kv, middle], local_sem.at[kv])
        )
    for copy in copies:
        copy.start()
    for kv in range(2):
        share(kv).start()

    @pl.when(has_up)
    def _():
        for kv in range(2):
            send_up(kv).start()

    @pl.when(has_down)
    def _():
        for kv in range(2):
            send_down(kv).start()

    @pl.when(has_far)
    def _():
        for group in range(GROUPS):
            send_query(group).start()

    @pl.when(root)
    def _():
        for kv in range(2):
            copies[1 + kv].wait()
        ids = anchor_ids[slot(x), :]
        token = lax.broadcasted_iota(jnp.int32, (SLOT, band), 1) + height_index * band
        selector = (ids[:, 0:band] == token).astype(partial.dtype)
        for kv in range(2):
            for part in range(YS):
                cut = slice(part * piece, (part + 1) * piece)
                partial[kv, :, cut] = jnp.dot(
                    selector, own[kv, band : 2 * band, cut], preferred_element_type=jnp.float32
                ).astype(partial.dtype)
        join_core().start()
        join_core().wait()
        for kv in range(2):
            picked[kv] = partial[kv] + mate_partial[kv]

    @pl.when(turn)
    def _():
        for group in range(GROUPS):
            turn_query(group).wait_recv()
            turn_query(group).start()

    @pl.when(face)
    def _():
        for kv in range(2):
            partial[kv] = picked[kv]
        join_far().start()
        join_far().wait()
        for kv in range(2):
            picked[kv] = picked[kv] + far_partial[kv]
        for d in range(1, YS):
            scatter(d).start()
        anchors[:, slot(x), 0:piece] = picked[:, :, 0:piece]

    @pl.when(hub & jnp.logical_not(root))
    def _():
        scatter_arrived = anchors.at[:, slot(x), quarter(y)]
        remote(SCATTER, scatter_arrived, scatter_arrived, y_peers[0]).wait_recv()

    @pl.when(hub)
    def _():
        for index in range(7):
            spread(index).start()

    @pl.when(leaf)
    def _():
        spread(0).wait_recv()

    @pl.when(active)
    def _():
        for d in range(1, YS):
            along_y(d).start()
        for d in range(1, YS):
            along_y(d, True).wait_recv()
        for d in range(1, XS):
            along_x(d).start()
        to_mate(0).start()
        for d in range(1, XS):
            along_x(d, True).wait_recv()
            to_mate(d).start()

    @pl.when(jnp.logical_not(has_down))
    def _():
        for ref in (own, mate):
            ref[:, 0:band, :] = jnp.zeros((2, band, feat), ref.dtype)

    @pl.when(jnp.logical_not(has_up))
    def _():
        for ref in (own, mate):
            ref[:, tokens + band : tokens + 2 * band, :] = jnp.zeros((2, band, feat), ref.dtype)

    @pl.when(jnp.logical_not(has_far))
    def _():
        far_part[...] = jnp.zeros(far_part.shape, far_part.dtype)
        far_stat[...] = jnp.full(far_stat.shape, MASKED, far_stat.dtype)

    span = 3 * band
    query_token = lax.broadcasted_iota(jnp.int32, (band, span), 0)
    key_token = lax.broadcasted_iota(jnp.int32, (band, span), 1)
    query_row, query_col = query_token // cols, lax.rem(query_token, cols)
    key_frame = key_token // band
    key_row = lax.rem(key_token, band) // cols
    key_col = lax.rem(key_token, cols)
    near = jnp.abs(query_col - key_col) <= REACH
    behind = jnp.where(core == 0, query_row - key_row, key_row - query_row)
    for frame in range(frames):
        moment = time_index * frames + frame - 1 + key_frame
        valid = near & (moment >= 0) & (moment < tm_count * frames)
        near_bias[frame] = jnp.where(valid, 0.0, MASKED)
        cross_bias[frame] = jnp.where(valid & (behind >= 0), 0.0, MASKED)

    @pl.when(has_down)
    def _():
        for kv in range(2):
            send_up(kv).wait_recv()
            pass_first(kv).start()

    @pl.when(has_up)
    def _():
        for kv in range(2):
            send_down(kv).wait_recv()
            pass_last(kv).start()

    copies[0].wait()

    @pl.when(jnp.logical_not(root))
    def _():
        for kv in range(2):
            copies[1 + kv].wait()

    def scores(query, keys):
        return scale * lax.dot_general(
            query, keys, (((1,), (1,)), ((), ())), preferred_element_type=jnp.float32
        )

    def weighted(weights, values):
        return jnp.dot(weights.astype(values.dtype), values, preferred_element_type=jnp.float32)

    lane = lax.broadcasted_iota(jnp.int32, (band, size), 1)

    def far_block(group, step):
        head, frame = step // frames, lax.rem(step, frames)
        cut = pl.ds(pl.multiple_of((group * per_group + head) * size, size), size)
        here = pl.ds(pl.multiple_of(frame * band, band), band)
        around = pl.ds(pl.multiple_of(frame * band, band), span)
        score = scores(far_queries[here, cut], own[0, around, cut]) + cross_bias[frame]
        top = jnp.max(score, axis=1, keepdims=True)
        weights = jnp.exp2(score - top)
        total = jnp.sum(weights, axis=1, keepdims=True)
        part = weighted(weights, own[1, around, cut]) / total
        sent_part[here, cut] = part.astype(sent_part.dtype)
        level = top + jnp.log(total) * LOG2E
        stat_block[here, :] = jnp.where(lane == head, level, stat_block[here, :])

    @pl.when(has_far)
    def _():
        stat_block[...] = jnp.zeros(stat_block.shape, stat_block.dtype)
        for group in range(GROUPS):
            send_query(group).wait_recv()

            @pl.loop(0, frames * per_group)
            def _(step):
                far_block(group, step)

            sent_stat[group] = jnp.transpose(stat_block[...])[0:8]
            send_part(group).start()
            send_stat(group).start()

    for kv in range(2):
        share(kv).wait_recv()

    @pl.when(has_down)
    def _():
        for kv in range(2):
            pass_first(kv).wait_recv()

    @pl.when(has_up)
    def _():
        for kv in range(2):
            pass_last(kv).wait_recv()

    @pl.when(jnp.logical_not(active))
    def _():
        for d in range(XS):
            to_mate(d).wait_recv()

    held = lax.rem(lax.broadcasted_iota(jnp.int32, (1, XS * SLOT), 1), SLOT)
    anchor_bias = jnp.where(held < 24, 0.0, MASKED)

    @pl.loop(0, frames * HEADS)
    def _(step):
        head, frame = step // frames, lax.rem(step, frames)
        cut = pl.ds(pl.multiple_of(head * size, size), size)
        here = pl.ds(pl.multiple_of(frame * band, band), band)
        around = pl.ds(pl.multiple_of(frame * band, band), span)
        query = own_queries[here, cut]
        near_score = scores(query, own[0, around, cut]) + near_bias[frame]
        cross_score = scores(query, mate[0, around, cut]) + cross_bias[frame]
        anchor_score = scores(query, anchors[0, :, cut]) + anchor_bias
        top = jnp.maximum(
            jnp.maximum(
                jnp.max(near_score, axis=1, keepdims=True),
                jnp.max(cross_score, axis=1, keepdims=True),
            ),
            jnp.max(anchor_score, axis=1, keepdims=True),
        )
        near_weights = jnp.exp2(near_score - top)
        cross_weights = jnp.exp2(cross_score - top)
        anchor_weights = jnp.exp2(anchor_score - top)
        total = (
            jnp.sum(near_weights, axis=1, keepdims=True)
            + jnp.sum(cross_weights, axis=1, keepdims=True)
            + jnp.sum(anchor_weights, axis=1, keepdims=True)
        )
        summed = (
            weighted(near_weights, own[1, around, cut])
            + weighted(cross_weights, mate[1, around, cut])
            + weighted(anchor_weights, anchors[1, :, cut])
        )
        result[here, cut] = summed / total
        own_level[here, cut] = jnp.broadcast_to(top + jnp.log(total) * LOG2E, (band, size))

    for group in range(GROUPS):

        @pl.when(has_far)
        def _():
            send_part(group).wait_recv()
            send_stat(group).wait_recv()

        stats = jnp.transpose(far_stat[group])
        for head in range(per_group):
            cut = pl.ds((group * per_group + head) * size, size)
            far_level = stats[0:tokens, head : head + 1]
            mine = own_level[:, cut]
            top = jnp.maximum(mine, far_level)
            mine = jnp.exp2(mine - top)
            other = jnp.exp2(far_level - top)
            mixed = mine * result[:, cut] + other * far_part[:, cut].astype(jnp.float32)
            out[:, cut] = (mixed / (mine + other)).astype(out.dtype)

    for kv in range(2):
        share(kv).wait_send()

    @pl.when(has_up)
    def _():
        for kv in range(2):
            send_up(kv).wait_send()
            pass_last(kv).wait_send()

    @pl.when(has_down)
    def _():
        for kv in range(2):
            send_down(kv).wait_send()
            pass_first(kv).wait_send()

    @pl.when(turn)
    def _():
        for group in range(GROUPS):
            turn_query(group).wait_send()

    @pl.when(face)
    def _():
        for d in range(1, YS):
            scatter(d).wait_send()

    @pl.when(hub)
    def _():
        for index in range(7):
            spread(index).wait_send()

    @pl.when(active)
    def _():
        for d in range(1, YS):
            along_y(d).wait_send()
        for d in range(1, XS):
            along_x(d).wait_send()
        for d in range(XS):
            to_mate(d).wait_send()

    @pl.when(has_far)
    def _():
        for group in range(GROUPS):
            send_query(group).wait_send()
            send_part(group).wait_send()
            send_stat(group).wait_send()


def per_device(tm_count, height_count, queries, keys_values, anchor_ids):
    frames, rows, cols, feat = queries.shape
    band = rows * cols
    tokens = frames * band
    size = feat // HEADS
    padded = -(-tokens // 128) * 128
    ids = jnp.pad(anchor_ids.reshape(XS, -1), ((0, 0), (0, SLOT - 24)), constant_values=-1)
    ids = jnp.broadcast_to(ids.reshape(XS * SLOT, 1), (XS * SLOT, 128))

    kernel = functools.partial(attention_kernel, frames, rows, cols, tm_count, height_count)
    bf16, f32 = jnp.bfloat16, jnp.float32
    out = pl.pallas_call(
        kernel,
        out_shape=jax.ShapeDtypeStruct((tokens, feat), bf16),
        in_specs=[
            pl.BlockSpec(memory_space=pl.ANY),
            pl.BlockSpec(memory_space=pl.ANY),
            pl.BlockSpec(memory_space=pltpu.VMEM),
        ],
        out_specs=pl.BlockSpec(memory_space=pltpu.VMEM),
        scratch_shapes=[
            pltpu.VMEM((2, tokens + 2 * band, feat), bf16),
            pltpu.VMEM((2, tokens + 2 * band, feat), bf16),
            pltpu.VMEM((tokens, feat), bf16),
            pltpu.VMEM((tokens, feat), bf16),
            pltpu.VMEM((tokens, feat), bf16),
            pltpu.VMEM((tokens, feat), bf16),
            pltpu.VMEM((GROUPS, 8, padded), f32),
            pltpu.VMEM((GROUPS, 8, padded), f32),
            pltpu.VMEM((tokens, feat), f32),
            pltpu.VMEM((tokens, feat), f32),
            pltpu.VMEM((frames, band, 3 * band), f32),
            pltpu.VMEM((frames, band, 3 * band), f32),
            pltpu.VMEM((padded, size), f32),
            pltpu.VMEM((2, SLOT, feat), bf16),
            pltpu.VMEM((2, SLOT, feat), bf16),
            pltpu.VMEM((2, SLOT, feat), bf16),
            pltpu.VMEM((2, SLOT, feat), bf16),
            pltpu.VMEM((2, XS * SLOT, feat), bf16),
            pltpu.SemaphoreType.DMA((TRANSFERS,)),
            pltpu.SemaphoreType.DMA((TRANSFERS,)),
            pltpu.SemaphoreType.DMA((3,)),
        ],
        compiler_params=pltpu.CompilerParams(
            collective_id=0, has_side_effects=True, vmem_limit_bytes=60 * 1024 * 1024
        ),
        name="attention",
    )(queries.reshape(tokens, feat), keys_values.reshape(2, tokens, feat), ids)
    return out.reshape(frames, rows, cols, feat)


def solution(mesh):
    body = functools.partial(per_device, mesh.shape["tm"], mesh.shape["height"])
    return jax.shard_map(
        body,
        mesh=mesh,
        in_specs=(P("tm", "height", None, None), P(None, "tm", "height", None, None), P()),
        out_specs=P("tm", "height", None, None),
        check_vma=False,
    )
```

```python
import functools

import jax
import jax.numpy as jnp
from jax import lax
from jax.experimental import pallas as pl
from jax.experimental.pallas import tpu as pltpu
from jax.sharding import PartitionSpec as P

HEADS = 20
GROUPS = 5
REACH = 3
LOG2E = 1.4426950408889634
MASKED = -1e30
MESH = pl.DeviceIdType.MESH

CORE, UP, DOWN, PASS_UP, PASS_DOWN, QUERY = 0, 2, 4, 6, 8, 10
PART = QUERY + GROUPS
STAT = PART + GROUPS
PAIRS = (GROUPS + 1) // 2
JOIN = STAT + PAIRS
SCATTER = JOIN + 2
SPREAD = SCATTER + 4
ALONG_Y = SPREAD + 8
ALONG_X = ALONG_Y + 4
TO_MATE = ALONG_X + 4
TRANSFERS = TO_MATE + 4

XS, YS, Z_LO = 4, 4, 8
SLOT = 32


def attention_kernel(
    frames, rows, cols, tm_count, height_count,
    queries, keys_values, anchor_ids, out,
    own, mate, own_queries, far_queries, sent_part, far_part, sent_stat, far_stat,
    result, own_level, near_bias, cross_bias, stat_block,
    partial, mate_partial, far_partial, picked, anchors, send_sem, recv_sem, local_sem,
):
    band = rows * cols
    tokens = frames * band
    feat = queries.shape[1]
    size = feat // HEADS
    per_group = HEADS // GROUPS
    width = per_group * size
    scale = LOG2E / size**0.5

    time_index = lax.axis_index("tm")
    height_index = lax.axis_index("height")
    core = lax.rem(height_index, 2)
    has_down = time_index > 0
    has_up = time_index < tm_count - 1
    has_far = ((core == 0) & (height_index > 0)) | ((core == 1) & (height_index < height_count - 1))
    core_mate = (time_index, height_index + 1 - 2 * core)
    far_mate = (time_index, jnp.clip(height_index - 1 + 2 * core, 0, height_count - 1))
    below = (jnp.maximum(time_index - 1, 0), height_index)
    above = (jnp.minimum(time_index + 1, tm_count - 1), height_index)

    bent = ((height_index == 4) | (height_index == height_count - 5))
    turn = jnp.logical_not(has_far)
    bend_end = (height_index == 3) | (height_index == height_count - 4)
    low = height_index < height_count // 2
    turn_id = (time_index, jnp.where(low, 0, height_count - 1))
    bent_id = (time_index, jnp.where(low, 4, height_count - 5))
    bend_end_id = (time_index, jnp.where(low, 3, height_count - 4))
    query_mate = (time_index, jnp.where(bent, turn_id[1], far_mate[1]))

    x, z_hi = height_index // 4, lax.rem(height_index // 2, 2)
    y, z_lo = time_index // Z_LO, lax.rem(time_index, Z_LO)
    active = core == 1 - z_hi
    hub = active & (z_lo == 0)
    root = time_index == 0
    face = hub & root
    leaf = active & (z_lo != 0)
    y_peers = [(lax.rem(y + d, YS) * Z_LO + z_lo, height_index) for d in range(1, YS)]
    x_peers = [
        (time_index, (lax.rem(x + d, XS) * 2 + z_hi) * 2 + core) for d in range(1, XS)
    ]

    leaves = [(y * Z_LO + d, height_index) for d in range(Z_LO - 1, 0, -1)]
    my_hub = (y * Z_LO, height_index)

    barrier = pltpu.get_barrier_semaphore()
    pl.semaphore_signal(barrier, inc=1, device_id=core_mate, device_id_type=MESH)
    for exists, mate_id in ((has_down, below), (has_up, above), (has_far, far_mate)):

        @pl.when(exists)
        def _():
            pl.semaphore_signal(barrier, inc=1, device_id=mate_id, device_id_type=MESH)

    for exists, group in (
        (active, y_peers + x_peers),
        (hub, leaves),
        (leaf, [my_hub]),
        (bent | bend_end, [turn_id]),
        (turn, [bent_id, bend_end_id]),
    ):

        @pl.when(exists)
        def _():
            for mate_id in group:
                pl.semaphore_signal(barrier, inc=1, device_id=mate_id, device_id_type=MESH)

    peers = 1 + sum(exists.astype(jnp.int32) for exists in (has_down, has_up, has_far, leaf))
    peers = peers + 6 * active.astype(jnp.int32) + 7 * hub.astype(jnp.int32)
    peers = peers + (bent | bend_end).astype(jnp.int32) + 2 * turn.astype(jnp.int32)
    pl.semaphore_wait(barrier, peers)

    def remote(index, src, dst, device, arrival=None):
        arrival = index if arrival is None else arrival
        return pltpu.make_async_remote_copy(
            src_ref=src, dst_ref=dst, send_sem=send_sem.at[index], recv_sem=recv_sem.at[arrival],
            device_id=device, device_id_type=MESH,
        )

    first, last = pl.ds(0, band), pl.ds(tokens + band, band)
    middle = pl.ds(band, tokens)

    def share(kv):
        return remote(CORE + kv, keys_values.at[kv], mate.at[kv, middle], core_mate)

    def send_up(kv):
        src = keys_values.at[kv, pl.ds(tokens - band, band)]
        return remote(UP + kv, src, own.at[kv, first], above)

    def send_down(kv):
        return remote(DOWN + kv, keys_values.at[kv, pl.ds(0, band)], own.at[kv, last], below)

    def pass_first(kv):
        return remote(PASS_UP + kv, own.at[kv, first], mate.at[kv, first], core_mate)

    def pass_last(kv):
        return remote(PASS_DOWN + kv, own.at[kv, last], mate.at[kv, last], core_mate)

    def columns(group):
        return pl.ds(group * width, width)

    def send_query(group):
        cut = columns(group)
        return remote(QUERY + group, queries.at[:, cut], far_queries.at[:, cut], query_mate)

    def turn_query(group):
        here = far_queries.at[:, columns(group)]
        return remote(QUERY + group, here, here, bend_end_id)

    def send_part(group):
        cut = columns(group)
        return remote(PART + group, sent_part.at[:, cut], far_part.at[:, cut], far_mate)

    def send_stat(pair):
        return remote(STAT + pair, sent_stat.at[pair], far_stat.at[pair], far_mate)

    def slot(index):
        return pl.ds(pl.multiple_of(index * SLOT, SLOT), SLOT)

    piece = feat // YS

    def quarter(index):
        return pl.ds(pl.multiple_of(index * piece, piece), piece)

    def join_core():
        return remote(JOIN, partial, mate_partial, core_mate)

    def join_far():
        return remote(JOIN + 1, partial, far_partial, far_mate)

    def scatter(d):
        cut = quarter(lax.rem(y + d, YS))
        src, dst = picked.at[:, :, cut], anchors.at[:, slot(x), cut]
        return remote(SCATTER + d, src, dst, y_peers[d - 1], SCATTER)

    def spread(index):
        here = anchors.at[:, slot(x), quarter(y)]
        return remote(SPREAD + index, here, here, leaves[index], SPREAD)

    def along_y(d, arriving=False):
        here = anchors.at[:, slot(x), quarter(lax.rem(y + YS - d, YS) if arriving else y)]
        return remote(ALONG_Y + d, here, here, y_peers[d - 1])

    def along_x(d, arriving=False):
        here = anchors.at[:, slot(lax.rem(x + XS - d, XS) if arriving else x)]
        return remote(ALONG_X + d, here, here, x_peers[d - 1])

    def to_mate(d):
        here = anchors.at[:, slot(lax.rem(x + XS - d, XS))]
        return remote(TO_MATE + d, here, here, core_mate)

    copies = [pltpu.make_async_copy(queries, own_queries, local_sem.at[2])]
    for kv in range(2):
        copies.append(
            pltpu.make_async_copy(keys_values.at[kv], own.at[kv, middle], local_sem.at[kv])
        )
    for copy in copies:
        copy.start()
    for kv in range(2):
        share(kv).start()

    @pl.when(has_up)
    def _():
        for kv in range(2):
            send_up(kv).start()

    @pl.when(has_down)
    def _():
        for kv in range(2):
            send_down(kv).start()

    @pl.when(has_far)
    def _():
        for group in range(GROUPS):
            send_query(group).start()

    @pl.when(root)
    def _():
        for kv in range(2):
            copies[1 + kv].wait()
        ids = anchor_ids[slot(x), :]
        token = lax.broadcasted_iota(jnp.int32, (SLOT, band), 1) + height_index * band
        selector = (ids[:, 0:band] == token).astype(partial.dtype)
        for kv in range(2):
            for part in range(YS):
                cut = slice(part * piece, (part + 1) * piece)
                partial[kv, :, cut] = jnp.dot(
                    selector, own[kv, band : 2 * band, cut], preferred_element_type=jnp.float32
                ).astype(partial.dtype)
        join_core().start()
        join_core().wait()
        for kv in range(2):
            picked[kv] = partial[kv] + mate_partial[kv]

    @pl.when(turn)
    def _():
        for group in range(GROUPS):
            turn_query(group).wait_recv()
            turn_query(group).start()

    @pl.when(face)
    def _():
        for kv in range(2):
            partial[kv] = picked[kv]
        join_far().start()
        join_far().wait()
        for kv in range(2):
            picked[kv] = picked[kv] + far_partial[kv]
        for d in range(1, YS):
            scatter(d).start()
        anchors[:, slot(x), 0:piece] = picked[:, :, 0:piece]

    @pl.when(hub & jnp.logical_not(root))
    def _():
        scatter_arrived = anchors.at[:, slot(x), quarter(y)]
        remote(SCATTER, scatter_arrived, scatter_arrived, y_peers[0]).wait_recv()

    @pl.when(hub)
    def _():
        for index in range(7):
            spread(index).start()

    @pl.when(leaf)
    def _():
        spread(0).wait_recv()

    @pl.when(active)
    def _():
        for d in range(1, YS):
            along_y(d).start()
        for d in range(1, YS):
            along_y(d, True).wait_recv()
        for d in range(1, XS):
            along_x(d).start()
        to_mate(0).start()
        for d in range(1, XS):
            along_x(d, True).wait_recv()
            to_mate(d).start()

    @pl.when(jnp.logical_not(has_down))
    def _():
        for ref in (own, mate):
            ref[:, 0:band, :] = jnp.zeros((2, band, feat), ref.dtype)

    @pl.when(jnp.logical_not(has_up))
    def _():
        for ref in (own, mate):
            ref[:, tokens + band : tokens + 2 * band, :] = jnp.zeros((2, band, feat), ref.dtype)

    @pl.when(jnp.logical_not(has_far))
    def _():
        far_part[...] = jnp.zeros(far_part.shape, far_part.dtype)
        far_stat[...] = jnp.full(far_stat.shape, MASKED, far_stat.dtype)

    span = 3 * band
    query_token = lax.broadcasted_iota(jnp.int32, (band, span), 0)
    key_token = lax.broadcasted_iota(jnp.int32, (band, span), 1)
    query_row, query_col = query_token // cols, lax.rem(query_token, cols)
    key_frame = key_token // band
    key_row = lax.rem(key_token, band) // cols
    key_col = lax.rem(key_token, cols)
    near = jnp.abs(query_col - key_col) <= REACH
    behind = jnp.where(core == 0, query_row - key_row, key_row - query_row)
    for frame in range(frames):
        moment = time_index * frames + frame - 1 + key_frame
        valid = near & (moment >= 0) & (moment < tm_count * frames)
        near_bias[frame] = jnp.where(valid, 0.0, MASKED)
        cross_bias[frame] = jnp.where(valid & (behind >= 0), 0.0, MASKED)

    @pl.when(has_down)
    def _():
        for kv in range(2):
            send_up(kv).wait_recv()
            pass_first(kv).start()

    @pl.when(has_up)
    def _():
        for kv in range(2):
            send_down(kv).wait_recv()
            pass_last(kv).start()

    copies[0].wait()

    @pl.when(jnp.logical_not(root))
    def _():
        for kv in range(2):
            copies[1 + kv].wait()

    def scores(query, keys):
        return scale * lax.dot_general(
            query, keys, (((1,), (1,)), ((), ())), preferred_element_type=jnp.float32
        )

    def weighted(weights, values):
        return jnp.dot(weights.astype(values.dtype), values, preferred_element_type=jnp.float32)

    lane = lax.broadcasted_iota(jnp.int32, (band, size), 1)

    def far_block(group, step):
        head, frame = step // frames, lax.rem(step, frames)
        cut = pl.ds(pl.multiple_of((group * per_group + head) * size, size), size)
        here = pl.ds(pl.multiple_of(frame * band, band), band)
        around = pl.ds(pl.multiple_of(frame * band, band), span)
        score = scores(far_queries[here, cut], own[0, around, cut]) + cross_bias[frame]
        top = jnp.max(score, axis=1, keepdims=True)
        weights = jnp.exp2(score - top)
        total = jnp.sum(weights, axis=1, keepdims=True)
        part = weighted(weights, own[1, around, cut]) / total
        sent_part[here, cut] = part.astype(sent_part.dtype)
        level = top + jnp.log(total) * LOG2E
        place = group % 2 * per_group + head
        stat_block[here, :] = jnp.where(lane == place, level, stat_block[here, :])

    @pl.when(has_far)
    def _():
        stat_block[...] = jnp.zeros(stat_block.shape, stat_block.dtype)
        for group in range(GROUPS):
            send_query(group).wait_recv()

            @pl.loop(0, frames * per_group)
            def _(step):
                far_block(group, step)

            send_part(group).start()
            if group % 2 == 1 or group == GROUPS - 1:
                sent_stat[group // 2] = jnp.transpose(stat_block[...])[0:8]
                send_stat(group // 2).start()

    for kv in range(2):
        share(kv).wait_recv()

    @pl.when(has_down)
    def _():
        for kv in range(2):
            pass_first(kv).wait_recv()

    @pl.when(has_up)
    def _():
        for kv in range(2):
            pass_last(kv).wait_recv()

    @pl.when(jnp.logical_not(active))
    def _():
        for d in range(XS):
            to_mate(d).wait_recv()

    held = lax.rem(lax.broadcasted_iota(jnp.int32, (1, XS * SLOT), 1), SLOT)
    anchor_bias = jnp.where(held < 24, 0.0, MASKED)

    @pl.loop(0, frames * HEADS)
    def _(step):
        head, frame = step // frames, lax.rem(step, frames)
        cut = pl.ds(pl.multiple_of(head * size, size), size)
        here = pl.ds(pl.multiple_of(frame * band, band), band)
        around = pl.ds(pl.multiple_of(frame * band, band), span)
        query = own_queries[here, cut]
        near_score = scores(query, own[0, around, cut]) + near_bias[frame]
        cross_score = scores(query, mate[0, around, cut]) + cross_bias[frame]
        anchor_score = scores(query, anchors[0, :, cut]) + anchor_bias
        top = jnp.maximum(
            jnp.maximum(
                jnp.max(near_score, axis=1, keepdims=True),
                jnp.max(cross_score, axis=1, keepdims=True),
            ),
            jnp.max(anchor_score, axis=1, keepdims=True),
        )
        near_weights = jnp.exp2(near_score - top)
        cross_weights = jnp.exp2(cross_score - top)
        anchor_weights = jnp.exp2(anchor_score - top)
        total = (
            jnp.sum(near_weights, axis=1, keepdims=True)
            + jnp.sum(cross_weights, axis=1, keepdims=True)
            + jnp.sum(anchor_weights, axis=1, keepdims=True)
        )
        summed = (
            weighted(near_weights, own[1, around, cut])
            + weighted(cross_weights, mate[1, around, cut])
            + weighted(anchor_weights, anchors[1, :, cut])
        )
        result[here, cut] = summed / total
        own_level[here, cut] = jnp.broadcast_to(top + jnp.log(total) * LOG2E, (band, size))

    for group in range(GROUPS):

        @pl.when(has_far)
        def _():
            send_part(group).wait_recv()
            if group % 2 == 0:
                send_stat(group // 2).wait_recv()

        stats = jnp.transpose(far_stat[group // 2])
        for head in range(per_group):
            cut = pl.ds((group * per_group + head) * size, size)
            place = group % 2 * per_group + head
            far_level = stats[0:tokens, place : place + 1]
            mine = own_level[:, cut]
            top = jnp.maximum(mine, far_level)
            mine = jnp.exp2(mine - top)
            other = jnp.exp2(far_level - top)
            mixed = mine * result[:, cut] + other * far_part[:, cut].astype(jnp.float32)
            out[:, cut] = (mixed / (mine + other)).astype(out.dtype)

    for kv in range(2):
        share(kv).wait_send()

    @pl.when(has_up)
    def _():
        for kv in range(2):
            send_up(kv).wait_send()
            pass_last(kv).wait_send()

    @pl.when(has_down)
    def _():
        for kv in range(2):
            send_down(kv).wait_send()
            pass_first(kv).wait_send()

    @pl.when(turn)
    def _():
        for group in range(GROUPS):
            turn_query(group).wait_send()

    @pl.when(face)
    def _():
        for d in range(1, YS):
            scatter(d).wait_send()

    @pl.when(hub)
    def _():
        for index in range(7):
            spread(index).wait_send()

    @pl.when(active)
    def _():
        for d in range(1, YS):
            along_y(d).wait_send()
        for d in range(1, XS):
            along_x(d).wait_send()
        for d in range(XS):
            to_mate(d).wait_send()

    @pl.when(has_far)
    def _():
        for group in range(GROUPS):
            send_query(group).wait_send()
            send_part(group).wait_send()
        for pair in range(PAIRS):
            send_stat(pair).wait_send()


def per_device(tm_count, height_count, queries, keys_values, anchor_ids):
    frames, rows, cols, feat = queries.shape
    band = rows * cols
    tokens = frames * band
    size = feat // HEADS
    padded = -(-tokens // 128) * 128
    ids = jnp.pad(anchor_ids.reshape(XS, -1), ((0, 0), (0, SLOT - 24)), constant_values=-1)
    ids = jnp.broadcast_to(ids.reshape(XS * SLOT, 1), (XS * SLOT, 128))

    kernel = functools.partial(attention_kernel, frames, rows, cols, tm_count, height_count)
    bf16, f32 = jnp.bfloat16, jnp.float32
    out = pl.pallas_call(
        kernel,
        out_shape=jax.ShapeDtypeStruct((tokens, feat), bf16),
        in_specs=[
            pl.BlockSpec(memory_space=pl.ANY),
            pl.BlockSpec(memory_space=pl.ANY),
            pl.BlockSpec(memory_space=pltpu.VMEM),
        ],
        out_specs=pl.BlockSpec(memory_space=pltpu.VMEM),
        scratch_shapes=[
            pltpu.VMEM((2, tokens + 2 * band, feat), bf16),
            pltpu.VMEM((2, tokens + 2 * band, feat), bf16),
            pltpu.VMEM((tokens, feat), bf16),
            pltpu.VMEM((tokens, feat), bf16),
            pltpu.VMEM((tokens, feat), bf16),
            pltpu.VMEM((tokens, feat), bf16),
            pltpu.VMEM((PAIRS, 8, padded), f32),
            pltpu.VMEM((PAIRS, 8, padded), f32),
            pltpu.VMEM((tokens, feat), f32),
            pltpu.VMEM((tokens, feat), f32),
            pltpu.VMEM((frames, band, 3 * band), f32),
            pltpu.VMEM((frames, band, 3 * band), f32),
            pltpu.VMEM((padded, size), f32),
            pltpu.VMEM((2, SLOT, feat), bf16),
            pltpu.VMEM((2, SLOT, feat), bf16),
            pltpu.VMEM((2, SLOT, feat), bf16),
            pltpu.VMEM((2, SLOT, feat), bf16),
            pltpu.VMEM((2, XS * SLOT, feat), bf16),
            pltpu.SemaphoreType.DMA((TRANSFERS,)),
            pltpu.SemaphoreType.DMA((TRANSFERS,)),
            pltpu.SemaphoreType.DMA((3,)),
        ],
        compiler_params=pltpu.CompilerParams(
            collective_id=0, has_side_effects=True, vmem_limit_bytes=60 * 1024 * 1024
        ),
        name="attention",
    )(queries.reshape(tokens, feat), keys_values.reshape(2, tokens, feat), ids)
    return out.reshape(frames, rows, cols, feat)


def solution(mesh):
    body = functools.partial(per_device, mesh.shape["tm"], mesh.shape["height"])
    return jax.shard_map(
        body,
        mesh=mesh,
        in_specs=(P("tm", "height", None, None), P(None, "tm", "height", None, None), P()),
        out_specs=P("tm", "height", None, None),
        check_vma=False,
    )
```
